512 devices in a mesh: dp: 16 (over z_hi, y), context: 32 (over z_lo, x, core).
Axes of the slice: x: 4, y: 8, z: 8 (z_hi: 2, z_lo: 4; z = z_hi * 4 + z_lo), core: 2. Of those that a mesh axis runs over, the one named last changes fastest.
Arguments:
- values: float32 [16, 256, 4096], P('dp', None, 'context'), may hold values from -6 to 6
- in_gate: float32 [16, 256, 4096], P('dp', None, 'context'), may hold values from -6 to 6
- out_gate: float32 [16, 256, 4096], P('dp', None, 'context'), may hold values from -6 to 6
- target: float32 [16, 256, 4096], P('dp', None, 'context'), may hold values from -6 to 6
- tap_param: float32 [256, 4096], P('context', 'dp'), may hold values from -6 to 6
- skip: float32 [256], replicated, may hold values from 0.1 to 1.9
Outputs:
- grad_values: float32 [16, 256, 4096], P('dp', None, 'context')
- tap_grad: float32 [256, 4096], P('context', 'dp')
The draws below stay inside these ranges and needn't reach their ends.
All inputs are finite; a program needn't handle non-finite values.
Results may differ from the reference program's by a relative error of at most 0.0003.
Values sent between devices are 32-bit elements; how exact they have to be, the bound alone decides.
A program may use at most 64 MiB of HBM per device.

```python
import jax
import jax.numpy as jnp
from jax import lax

CH = 256
SEQ = 4096
BATCH = 16


def level_of(own_key, extent, shards, low, largest):
    def one(axis_at, parts):
        draws = jax.random.uniform(jax.random.fold_in(jax.random.fold_in(own_key, 6), axis_at), (parts,), jnp.float32, low / len(shards), largest / len(shards))
        return jnp.repeat(jnp.exp(draws), extent[axis_at] // parts).reshape((-1,) + (1,) * (len(extent) - axis_at - 1))

    factor_of = one(*shards[0])
    for cut in shards[1:]:
        factor_of = factor_of * one(*cut)
    return factor_of


def scatter_about(own_key, shape, deviation, reach, shards=(), dtype=jnp.bfloat16):
    drawn = jax.random.normal(own_key, shape, jnp.float32) * deviation
    if len(shards) > 0:
        drawn = level_of(own_key, shape, shards, -0.22, 0.18) * drawn
    return jnp.clip(drawn, min=-reach, max=reach).astype(dtype)


def setup_inputs(seed: int = 0) -> dict:
    keys = jax.random.split(jax.random.key(seed), 7)
    values = scatter_about(keys[0], (BATCH, CH, SEQ), 1.0, 6.0, ((0, 16), (2, 32)), jnp.float32)
    in_gate = scatter_about(keys[1], (BATCH, CH, SEQ), 1.0, 6.0, ((0, 16), (2, 32)), jnp.float32)
    out_gate = scatter_about(keys[2], (BATCH, CH, SEQ), 1.0, 6.0, ((0, 16), (2, 32)), jnp.float32)
    target = scatter_about(keys[3], (BATCH, CH, SEQ), 1.0, 6.0, ((0, 16), (2, 32)), jnp.float32)
    tap_param = scatter_about(keys[4], (CH, SEQ), 1.0, 6.0, ((0, 32), (1, 16)), jnp.float32)
    skip = jnp.clip(1.0 + 0.18 * jax.random.normal(keys[5], (CH,), jnp.float32), 0.1, 1.9)
    return {"values": values, "in_gate": in_gate, "out_gate": out_gate, "target": target, "tap_param": tap_param, "skip": skip}


def reference(values, in_gate, out_gate, target, tap_param, skip):
    length = 2 * SEQ
    taps = tap_param * SEQ ** -0.5
    tap_spec = jnp.fft.rfft(taps, n=length)
    skip_col = skip[:, None]

    def one_sequence(carry, items):
        stream, gate_in, gate_out, goal = items
        mixed = stream * gate_in
        mixed_spec = jnp.fft.rfft(mixed, n=length)
        conv = jnp.fft.irfft(mixed_spec * tap_spec, n=length)[:, :SEQ]
        middle = conv + skip_col * mixed
        grad_out = gate_out * (gate_out * middle - goal)
        grad_spec = jnp.fft.rfft(grad_out, n=length)
        back = jnp.fft.irfft(grad_spec * jnp.conj(tap_spec), n=length)[:, :SEQ]
        tap_part = jnp.fft.irfft(grad_spec * jnp.conj(mixed_spec), n=length)[:, :SEQ]
        return carry + tap_part, gate_in * (back + skip_col * grad_out)

    total, grad_values = lax.scan(one_sequence, jnp.zeros_like(tap_param), (values, in_gate, out_gate, target))
    tap_grad = total * (SEQ * BATCH) ** -0.5
    return grad_values, tap_grad
```

```python
import functools
import math

import jax
import jax.numpy as jnp
import numpy as np
from jax import lax
from jax.experimental import pallas as pl
from jax.experimental.pallas import tpu as pltpu
from jax.sharding import PartitionSpec as P

MESH = pl.DeviceIdType.MESH
NB = 32
LANES = 128
CPD = 8
NY = 8
SEQ = NB * LANES
TAPS = 2 * LANES


def leaf_angles(theta, length):
    if length == 1:
        return [theta]
    return leaf_angles(theta / 2, length // 2) + leaf_angles(theta / 2 + math.pi, length // 2)


@functools.cache
def tables():
    order = np.array([round((a * 64 / (2 * math.pi) - 0.5) / 2) % NB for a in leaf_angles(math.pi / 2, NB)])
    r = np.arange(LANES)
    angle = 2 * math.pi * (2 * order[:, None] + 0.5) * r[None, :] / (2 * SEQ)
    turn = 2 * math.pi * (r[:, None] * r[None, :] % LANES) / LANES
    c, s = np.cos(turn), np.sin(turn)
    w = np.block([[c, -s], [s, c]]).astype(np.float32)
    w_hi = w.astype(jnp.bfloat16)
    w_lo = (w - w_hi.astype(np.float32)).astype(jnp.bfloat16)
    return (
        np.cos(angle).astype(np.float32)[:, None, :],
        np.sin(angle).astype(np.float32)[:, None, :],
        w_hi,
        w_lo,
    )


def evaluate(re, im, theta):
    length = re.shape[0]
    if length == 1:
        return [(re, im)]
    half = length // 2
    c, s = math.cos(theta / 2), math.sin(theta / 2)
    if im is None:
        t_re, t_im = c * re[half:], -s * re[half:]
        low = (re[:half] + t_re, t_im)
        high = (re[:half] - t_re, -t_im)
    else:
        t_re = c * re[half:] + s * im[half:]
        t_im = c * im[half:] - s * re[half:]
        low = (re[:half] + t_re, im[:half] + t_im)
        high = (re[:half] - t_re, im[:half] - t_im)
    return evaluate(*low, theta / 2) + evaluate(*high, theta / 2 + math.pi)


def gather_back(re, im, theta, real_only):
    length = re.shape[0]
    if length == 1:
        return re, im
    half = length // 2
    a_re, a_im = gather_back(re[:half], im[:half], theta / 2, False)
    b_re, b_im = gather_back(re[half:], im[half:], theta / 2 + math.pi, False)
    c, s = math.cos(theta / 2), math.sin(theta / 2)
    d_re, d_im = a_re - b_re, a_im - b_im
    top = c * d_re - s * d_im
    if real_only:
        return jnp.concatenate([a_re + b_re, top], axis=0), None
    return jnp.concatenate([a_re + b_re, top], axis=0), jnp.concatenate([a_im + b_im, c * d_im + s * d_re], axis=0)


def lane_transform(left, right, w_hi, w_lo):
    joined = jnp.concatenate([left, right], axis=1)
    hi = joined.astype(jnp.bfloat16)
    lo = (joined - hi.astype(jnp.float32)).astype(jnp.bfloat16)
    dot = functools.partial(jnp.dot, preferred_element_type=jnp.float32)
    out = dot(hi, w_hi[...]) + (dot(lo, w_hi[...]) + dot(hi, w_lo[...]))
    return out[:, :LANES], out[:, LANES:]


def forward(x, tcos, tsin, w_hi, w_lo):
    leaves = evaluate(x, None, math.pi / 2)
    re = jnp.concatenate([leaf[0] for leaf in leaves], axis=0)
    im = jnp.concatenate([leaf[1] for leaf in leaves], axis=0)
    c, s = tcos[...], tsin[...]
    flat = (NB * CPD, LANES)
    return lane_transform((re * c + im * s).reshape(flat), (im * c - re * s).reshape(flat), w_hi, w_lo)


def inverse(re, im, tcos, tsin, w_hi, w_lo):
    b_im, b_re = lane_transform(im, re, w_hi, w_lo)
    b_im, b_re = b_im.reshape(NB, CPD, LANES), b_re.reshape(NB, CPD, LANES)
    c, s = tcos[...], tsin[...]
    return gather_back(b_re * c - b_im * s, b_im * c + b_re * s, math.pi / 2, True)[0]


def conj_mul(a, b):
    return a[0] * b[0] + a[1] * b[1], a[1] * b[0] - a[0] * b[1]


def kernel(
    values, in_gate, out_gate, target, tap_param, skip, tcos_h, tsin_h, whi_h, wlo_h,
    grad_values, tap_grad,
    v_val, v_gate, tcos, tsin, w_hi, w_lo,
    mix_send, mix, gate, goal, taps, conv, back_send, back, tap_send, tap_recv, pair_send, pair_recv,
    load_sem, send_sem, recv_sem,
):
    me_d, me = lax.axis_index("dp"), lax.axis_index("context")
    mz, my = me_d // NY, me_d % NY

    loads = [(values.at[0], v_val), (in_gate.at[0], v_gate), (tcos_h, tcos), (tsin_h, tsin), (whi_h, w_hi), (wlo_h, w_lo)]
    loads = [pltpu.make_async_copy(src, dst, load_sem.at[k]) for k, (src, dst) in enumerate(loads)]
    own_rows = pl.ds(pl.multiple_of(me * CPD, CPD), CPD)
    loads += [
        pltpu.make_async_copy(out_gate.at[0, own_rows], gate.at[me], load_sem.at[6]),
        pltpu.make_async_copy(target.at[0, own_rows], goal.at[me], load_sem.at[7]),
        pltpu.make_async_copy(tap_param, taps.at[mz, my], load_sem.at[8]),
    ]
    for load in loads:
        load.start()

    barrier = pltpu.get_barrier_semaphore()

    def greet(s, carry):
        pl.semaphore_signal(barrier, inc=1, device_id=(me_d, (me + s) % NB), device_id_type=MESH)
        return carry

    def greet_y(s, carry):
        pl.semaphore_signal(barrier, inc=1, device_id=(mz * NY + (my + s) % NY, me), device_id_type=MESH)
        return carry

    lax.fori_loop(1, NB, greet, 0)
    lax.fori_loop(1, NY, greet_y, 0)
    pair = (1 - mz) * NY + my
    pl.semaphore_signal(barrier, inc=1, device_id=(pair, me), device_id_type=MESH)
    pl.semaphore_wait(barrier, NB - 1 + NY - 1 + 1)

    def remote(src, dst, k, device):
        return pltpu.make_async_remote_copy(
            src_ref=src, dst_ref=dst, send_sem=send_sem.at[k], recv_sem=recv_sem.at[k], device_id=device, device_id_type=MESH
        )

    def whole(ref, k):
        return remote(ref, ref, k, (me_d, (me + 1) % NB))

    def rows(p):
        return pl.ds(pl.multiple_of(p * CPD, CPD), CPD)

    def spread(make, k):
        def step(s, carry):
            p = (me + s) % NB
            src, dst = make(p)
            remote(src, dst, k, (me_d, p)).start()
            return carry

        lax.fori_loop(1, NB, step, 0)

    def spread_y(make, k):
        def step(s, carry):
            y = (my + s) % NY
            src, dst = make(y)
            remote(src, dst, k, (mz * NY + y, me)).start()
            return carry

        lax.fori_loop(1, NY, step, 0)

    to_pair = remote(tap_param, taps.at[mz, my], 0, (pair, me))
    to_pair.start()
    loads[0].wait()
    loads[1].wait()
    mix_send[...] = (v_val[...] * v_gate[...]).reshape(NB, CPD, LANES)
    mix[me] = mix_send[me]
    spread(lambda p: (mix_send.at[p], mix.at[me]), 1)
    spread_y(lambda y: (tap_param, taps.at[mz, my]), 2)
    spread(lambda p: (out_gate.at[0, rows(p)], gate.at[me]), 3)
    spread(lambda p: (target.at[0, rows(p)], goal.at[me]), 4)
    to_pair.wait()
    spread_y(lambda y: (taps.at[1 - mz, my], taps.at[1 - mz, my]), 5)
    for load in loads[2:]:
        load.wait()

    lane_args = (tcos, tsin, w_hi, w_lo)
    whole(mix.at[pl.ds(0, NB - 1)], 1).wait()
    mix_spec = forward(mix[...], *lane_args)
    whole(taps.at[0, pl.ds(0, NY - 1)], 2).wait()
    whole(taps.at[0, pl.ds(0, NY - 1)], 5).wait()
    tap_all = taps[...].reshape(2 * NY, CPD, TAPS)
    tap_all = jnp.stack([tap_all[:, :, :LANES], tap_all[:, :, LANES:]], axis=1).reshape(NB, CPD, LANES)
    tap_spec = forward(tap_all * (SEQ**-0.5 / SEQ), *lane_args)
    product = (
        mix_spec[0] * tap_spec[0] - mix_spec[1] * tap_spec[1],
        mix_spec[0] * tap_spec[1] + mix_spec[1] * tap_spec[0],
    )
    row = lax.broadcasted_iota(jnp.int32, (CPD, LANES), 0)
    skip_tile = jnp.zeros((CPD, LANES), jnp.float32)
    for c in range(CPD):
        skip_tile = jnp.where(row == c, skip[me * CPD + c], skip_tile)
    conv[...] = inverse(*product, *lane_args) + skip_tile * mix[...]

    whole(gate.at[pl.ds(0, NB - 1)], 3).wait()
    whole(goal.at[pl.ds(0, NB - 1)], 4).wait()
    grad_out = gate[...] * (gate[...] * conv[...] - goal[...])
    conv[...] = grad_out
    grad_spec = forward(grad_out, *lane_args)

    tap_part = inverse(*conj_mul(grad_spec, mix_spec), *lane_args).reshape(2, NY, 2, CPD, LANES)
    for z in range(2):
        for half in range(2):
            tap_send[:, z, :, half * LANES : (half + 1) * LANES] = tap_part[z, :, half]
    tap_recv[my] = tap_send[my]
    spread_y(lambda y: (tap_send.at[y], tap_recv.at[my]), 6)

    back_send[...] = inverse(*conj_mul(grad_spec, tap_spec), *lane_args) + skip_tile * conv[...]
    back[me] = back_send[me]
    spread(lambda p: (back_send.at[p], back.at[me]), 7)

    whole(tap_recv.at[pl.ds(0, NY - 1)], 6).wait()
    total = jnp.sum(tap_recv[...], axis=0)
    pair_send[...] = total
    to_pair = remote(pair_send.at[1 - mz], pair_recv, 8, (pair, me))
    to_pair.start()

    whole(back.at[pl.ds(0, NB - 1)], 7).wait()
    grad_values[0] = v_gate[...] * back[...].reshape(NB * CPD, LANES)
    to_pair.wait()
    tap_grad[...] = (pair_send[mz] + pair_recv[...]) * ((SEQ * 2 * NY) ** -0.5 / SEQ)


def body(values, in_gate, out_gate, target, tap_param, skip):
    f32, bf16 = jnp.float32, jnp.bfloat16
    block = (NB, CPD, LANES)
    hbm = pl.BlockSpec(memory_space=pl.ANY)
    vmem = pl.BlockSpec(memory_space=pltpu.VMEM)
    constants = [jnp.asarray(t) for t in tables()]
    return pl.pallas_call(
        kernel,
        out_shape=(jax.ShapeDtypeStruct(values.shape, f32), jax.ShapeDtypeStruct(tap_param.shape, f32)),
        in_specs=[hbm] * 5 + [pl.BlockSpec(memory_space=pltpu.SMEM)] + [hbm] * 4,
        out_specs=(vmem, vmem),
        scratch_shapes=[
            pltpu.VMEM((NB * CPD, LANES), f32),
            pltpu.VMEM((NB * CPD, LANES), f32),
            pltpu.VMEM((NB, 1, LANES), f32),
            pltpu.VMEM((NB, 1, LANES), f32),
            pltpu.VMEM((2 * LANES, 2 * LANES), bf16),
            pltpu.VMEM((2 * LANES, 2 * LANES), bf16),
            pltpu.VMEM(block, f32),
            pltpu.VMEM(block, f32),
            pltpu.VMEM(block, f32),
            pltpu.VMEM(block, f32),
            pltpu.VMEM((2, NY, CPD, TAPS), f32),
            pltpu.VMEM(block, f32),
            pltpu.VMEM(block, f32),
            pltpu.VMEM(block, f32),
            pltpu.VMEM((NY, 2, CPD, TAPS), f32),
            pltpu.VMEM((NY, 2, CPD, TAPS), f32),
            pltpu.VMEM((2, CPD, TAPS), f32),
            pltpu.VMEM((CPD, TAPS), f32),
            pltpu.SemaphoreType.DMA((9,)),
            pltpu.SemaphoreType.DMA((9,)),
            pltpu.SemaphoreType.DMA((9,)),
        ],
        compiler_params=pltpu.CompilerParams(collective_id=0, has_side_effects=True, vmem_limit_bytes=60 * 1024 * 1024),
        cost_estimate=pl.CostEstimate(flops=2**30, bytes_accessed=2**20, transcendentals=0),
        name="gated_conv",
    )(values, in_gate, out_gate, target, tap_param, skip, *constants)


def solution(mesh):
    stream = P("dp", None, "context")
    return jax.shard_map(
        body,
        mesh=mesh,
        in_specs=(stream, stream, stream, stream, P("context", "dp"), P()),
        out_specs=(stream, P("context", "dp")),
        check_vma=False,
    )
```

```python
import functools
import math

import jax
import jax.numpy as jnp
import numpy as np
from jax import lax
from jax.experimental import pallas as pl
from jax.experimental.pallas import tpu as pltpu
from jax.sharding import PartitionSpec as P

MESH = pl.DeviceIdType.MESH
NB = 32
LANES = 128
CPD = 8
NY = 8
SEQ = NB * LANES
TAPS = 2 * LANES


def leaf_angles(theta, length):
    if length == 1:
        return [theta]
    return leaf_angles(theta / 2, length // 2) + leaf_angles(theta / 2 + math.pi, length // 2)


@functools.cache
def tables():
    order = np.array([round((a * 64 / (2 * math.pi) - 0.5) / 2) % NB for a in leaf_angles(math.pi / 2, NB)])
    r = np.arange(LANES)
    angle = 2 * math.pi * (2 * order[:, None] + 0.5) * r[None, :] / (2 * SEQ)
    turn = 2 * math.pi * (r[:, None] * r[None, :] % LANES) / LANES
    c, s = np.cos(turn), np.sin(turn)
    w = np.block([[c, -s], [s, c]]).astype(np.float32)
    w_hi = w.astype(jnp.bfloat16)
    w_lo = (w - w_hi.astype(np.float32)).astype(jnp.bfloat16)
    return (
        np.cos(angle).astype(np.float32)[:, None, :],
        np.sin(angle).astype(np.float32)[:, None, :],
        w_hi,
        w_lo,
    )


def evaluate(re, im, theta):
    length = re.shape[0]
    if length == 1:
        return [(re, im)]
    half = length // 2
    c, s = math.cos(theta / 2), math.sin(theta / 2)
    if im is None:
        t_re, t_im = c * re[half:], -s * re[half:]
        low = (re[:half] + t_re, t_im)
        high = (re[:half] - t_re, -t_im)
    else:
        t_re = c * re[half:] + s * im[half:]
        t_im = c * im[half:] - s * re[half:]
        low = (re[:half] + t_re, im[:half] + t_im)
        high = (re[:half] - t_re, im[:half] - t_im)
    return evaluate(*low, theta / 2) + evaluate(*high, theta / 2 + math.pi)


def gather_back(re, im, theta, real_only):
    length = re.shape[0]
    if length == 1:
        return re, im
    half = length // 2
    a_re, a_im = gather_back(re[:half], im[:half], theta / 2, False)
    b_re, b_im = gather_back(re[half:], im[half:], theta / 2 + math.pi, False)
    c, s = math.cos(theta / 2), math.sin(theta / 2)
    d_re, d_im = a_re - b_re, a_im - b_im
    top = c * d_re - s * d_im
    if real_only:
        return jnp.concatenate([a_re + b_re, top], axis=0), None
    return jnp.concatenate([a_re + b_re, top], axis=0), jnp.concatenate([a_im + b_im, c * d_im + s * d_re], axis=0)


def lane_transform(left, right, w_hi, w_lo):
    joined = jnp.concatenate([left, right], axis=1)
    hi = joined.astype(jnp.bfloat16)
    lo = (joined - hi.astype(jnp.float32)).astype(jnp.bfloat16)
    dot = functools.partial(jnp.dot, preferred_element_type=jnp.float32)
    out = dot(hi, w_hi[...]) + (dot(lo, w_hi[...]) + dot(hi, w_lo[...]))
    return out[:, :LANES], out[:, LANES:]


def forward(x, tcos, tsin, w_hi, w_lo):
    leaves = evaluate(x, None, math.pi / 2)
    re = jnp.concatenate([leaf[0] for leaf in leaves], axis=0)
    im = jnp.concatenate([leaf[1] for leaf in leaves], axis=0)
    c, s = tcos[...], tsin[...]
    flat = (NB * CPD, LANES)
    return lane_transform((re * c + im * s).reshape(flat), (im * c - re * s).reshape(flat), w_hi, w_lo)


def inverse(re, im, tcos, tsin, w_hi, w_lo):
    b_im, b_re = lane_transform(im, re, w_hi, w_lo)
    b_im, b_re = b_im.reshape(NB, CPD, LANES), b_re.reshape(NB, CPD, LANES)
    c, s = tcos[...], tsin[...]
    return gather_back(b_re * c - b_im * s, b_im * c + b_re * s, math.pi / 2, True)[0]


def conj_mul(a, b):
    return a[0] * b[0] + a[1] * b[1], a[1] * b[0] - a[0] * b[1]


def kernel(
    values, in_gate, out_gate, target, tap_param, skip, tcos_h, tsin_h, whi_h, wlo_h,
    back, tap_a, tap_b,
    v_val, v_gate, tcos, tsin, w_hi, w_lo,
    mix_send, mix, goal_send, goal, taps, grad, back_send, tap_send, tap_recv, pair_send,
    load_sem, send_sem, recv_sem,
):
    me_d, me = lax.axis_index("dp"), lax.axis_index("context")
    mz, my = me_d // NY, me_d % NY
    low, side, core = me // 8, me % 8 // 2, me % 2
    other = (1 - mz) * NY + my
    owned = (me + NB // 2) % NB
    barrier = pltpu.get_barrier_semaphore()

    def partner(j):
        flip = 3 - j // 8
        z = (low // 2 + flip // 2) % 2 * 2 + (low % 2 + flip % 2) % 2
        return z * 8 + (side + 3 - j % 8 // 2) % 4 * 2 + (core + 1 - j % 2) % 2

    def partner_y(k):
        half = k // 2
        return (my + 4 + (1 - k % 2) * half - k % 2 * (half + 1)) % NY

    def greet(j, carry):
        pl.semaphore_signal(barrier, inc=1, device_id=(me_d, partner(j)), device_id_type=MESH)
        return carry

    def greet_y(k, carry):
        pl.semaphore_signal(barrier, inc=1, device_id=(mz * NY + partner_y(k), me), device_id_type=MESH)
        return carry

    lax.fori_loop(0, NY - 1, greet_y, 0)
    pl.semaphore_signal(barrier, inc=1, device_id=(other, owned), device_id_type=MESH)
    lax.fori_loop(0, NB - 1, greet, 0)

    loads = [
        (values, v_val),
        (in_gate, v_gate),
        (out_gate, goal_send.at[:, 0]),
        (target, goal_send.at[:, 1]),
        (tcos_h, tcos),
        (tsin_h, tsin),
        (whi_h, w_hi),
        (wlo_h, w_lo),
    ]
    loads = [pltpu.make_async_copy(src, dst, load_sem.at[k]) for k, (src, dst) in enumerate(loads)]
    for load in loads:
        load.start()
    for load in loads[:2]:
        load.wait()
    mix_send[...] = v_val[...] * v_gate[...]
    for load in loads[2:4]:
        load.wait()
    pl.semaphore_wait(barrier, NB - 1 + NY - 1 + 1)

    def remote(src, dst, k, device):
        return pltpu.make_async_remote_copy(
            src_ref=src, dst_ref=dst, send_sem=send_sem.at[k], recv_sem=recv_sem.at[k], device_id=device, device_id_type=MESH
        )

    def whole(ref, k):
        return remote(ref, ref, k, (other, me))

    def spread(make, k):
        def step(j, carry):
            p = partner(j)
            src, dst = make(p)
            remote(src, dst, k, (me_d, p)).start()
            return carry

        lax.fori_loop(0, NB - 1, step, 0)

    def spread_y(make, k):
        def step(j, carry):
            y = partner_y(j)
            src, dst = make(y)
            remote(src, dst, k, (mz * NY + y, me)).start()
            return carry

        lax.fori_loop(0, NY - 1, step, 0)

    for z in range(2):
        remote(tap_param, taps.at[my, mz], 0, (z * NY + my, owned)).start()
    spread(lambda p: (mix_send.at[(p + NB // 2) % NB], mix.at[me]), 1)
    whole(taps.at[my], 0).wait()
    spread_y(lambda y: (taps.at[my], taps.at[my]), 2)
    spread(lambda p: (goal_send.at[(p + NB // 2) % NB], goal.at[me]), 7)
    mix[me] = mix_send[owned]
    goal[me] = goal_send[owned]
    for load in loads[4:]:
        load.wait()

    row = lax.broadcasted_iota(jnp.int32, (CPD, LANES), 0)
    skip_tile = jnp.zeros((CPD, LANES), jnp.float32)
    for c in range(CPD):
        skip_tile = jnp.where(row == c, skip[owned * CPD + c], skip_tile)

    lane_args = (tcos, tsin, w_hi, w_lo)
    whole(mix.at[pl.ds(0, NB - 1)], 1).wait()
    mixed = mix[...]
    mix_spec = forward(mixed, *lane_args)
    whole(taps.at[pl.ds(0, NY - 1)], 2).wait()
    tap_all = jnp.concatenate([taps[:, 0], taps[:, 1]], axis=0)
    tap_all = jnp.stack([tap_all[:, :, :LANES], tap_all[:, :, LANES:]], axis=1).reshape(NB, CPD, LANES)
    tap_spec = forward(tap_all * (SEQ**-0.5 / SEQ), *lane_args)
    product = (
        mix_spec[0] * tap_spec[0] - mix_spec[1] * tap_spec[1],
        mix_spec[0] * tap_spec[1] + mix_spec[1] * tap_spec[0],
    )
    grad[...] = inverse(*product, *lane_args) + skip_tile * mixed

    whole(goal.at[pl.ds(0, NB - 1)], 7).wait()
    gate = goal[:, 0]
    grad_out = gate * (gate * grad[...] - goal[:, 1])
    grad[...] = grad_out
    grad_spec = forward(grad_out, *lane_args)

    tap_part = inverse(*conj_mul(grad_spec, mix_spec), *lane_args).reshape(2, NY, 2, CPD, LANES)
    for z in range(2):
        for half in range(2):
            tap_send[:, z, :, half * LANES : (half + 1) * LANES] = tap_part[z, :, half]
    spread_y(lambda y: (tap_send.at[y], tap_recv.at[my]), 4)
    tap_recv[my] = tap_send[my]

    back_send[...] = inverse(*conj_mul(grad_spec, tap_spec), *lane_args) + skip_tile * grad[...]
    spread(lambda p: (back_send.at[p], back.at[owned]), 5)
    keep = pltpu.make_async_copy(back_send.at[me], back.at[owned], load_sem.at[0])
    keep.start()

    whole(tap_recv.at[pl.ds(0, NY - 1)], 4).wait()
    pair_send[...] = jnp.sum(tap_recv[...], axis=0)
    for z in range(2):

        @pl.when(mz == 0)
        def _():
            remote(pair_send.at[z], tap_a, 3, (z * NY + my, owned)).start()

        @pl.when(mz == 1)
        def _():
            remote(pair_send.at[z], tap_b, 6, (z * NY + my, owned)).start()

    keep.wait()
    whole(back.at[pl.ds(0, NB - 1)], 5).wait()
    whole(tap_a, 3).wait_recv()
    whole(tap_b, 6).wait_recv()

    @pl.when(mz == 0)
    def _():
        whole(pair_send, 3).wait_send()

    @pl.when(mz == 1)
    def _():
        whole(pair_send, 6).wait_send()


def finish_kernel(back, in_gate, tap_a, tap_b, grad_values, tap_grad):
    grad_values[...] = in_gate[...] * back[...]
    tap_grad[...] = (tap_a[...] + tap_b[...]) * ((SEQ * 2 * NY) ** -0.5 / SEQ)


def body(values, in_gate, out_gate, target, tap_param, skip):
    f32, bf16 = jnp.float32, jnp.bfloat16
    block = (NB, CPD, LANES)
    shape = values.shape
    hbm = pl.BlockSpec(memory_space=pl.ANY)
    vmem = pl.BlockSpec(memory_space=pltpu.VMEM)
    constants = [jnp.asarray(t) for t in tables()]
    values, in_gate, out_gate, target = [a.reshape(block) for a in (values, in_gate, out_gate, target)]
    tap_shape = jax.ShapeDtypeStruct(tap_param.shape, f32)
    back, tap_a, tap_b = pl.pallas_call(
        kernel,
        out_shape=(jax.ShapeDtypeStruct(block, f32), tap_shape, tap_shape),
        in_specs=[hbm] * 5 + [pl.BlockSpec(memory_space=pltpu.SMEM)] + [hbm] * 4,
        out_specs=(hbm, hbm, hbm),
        scratch_shapes=[
            pltpu.VMEM(block, f32),
            pltpu.VMEM(block, f32),
            pltpu.VMEM((NB, 1, LANES), f32),
            pltpu.VMEM((NB, 1, LANES), f32),
            pltpu.VMEM((2 * LANES, 2 * LANES), bf16),
            pltpu.VMEM((2 * LANES, 2 * LANES), bf16),
            pltpu.VMEM(block, f32),
            pltpu.VMEM(block, f32),
            pltpu.VMEM((NB, 2, CPD, LANES), f32),
            pltpu.VMEM((NB, 2, CPD, LANES), f32),
            pltpu.VMEM((NY, 2, CPD, TAPS), f32),
            pltpu.VMEM(block, f32),
            pltpu.VMEM(block, f32),
            pltpu.VMEM((NY, 2, CPD, TAPS), f32),
            pltpu.VMEM((NY, 2, CPD, TAPS), f32),
            pltpu.VMEM((2, CPD, TAPS), f32),
            pltpu.SemaphoreType.DMA((8,)),
            pltpu.SemaphoreType.DMA((8,)),
            pltpu.SemaphoreType.DMA((8,)),
        ],
        compiler_params=pltpu.CompilerParams(collective_id=0, has_side_effects=True, vmem_limit_bytes=56 * 1024 * 1024),
        cost_estimate=pl.CostEstimate(flops=2**30, bytes_accessed=2**20, transcendentals=0),
        name="gated_conv",
    )(values, in_gate, out_gate, target, tap_param, skip, *constants)
    grad_values, tap_grad = pl.pallas_call(
        finish_kernel,
        out_shape=(jax.ShapeDtypeStruct(block, f32), tap_shape),
        in_specs=[vmem] * 4,
        out_specs=(vmem, vmem),
        name="finish",
    )(back, in_gate, tap_a, tap_b)
    return grad_values.reshape(shape), tap_grad


def solution(mesh):
    stream = P("dp", None, "context")
    return jax.shard_map(
        body,
        mesh=mesh,
        in_specs=(stream, stream, stream, stream, P("context", "dp"), P()),
        out_specs=(stream, P("context", "dp")),
        check_vma=False,
    )
```

```python
import functools
import math

import jax
import jax.numpy as jnp
import numpy as np
from jax import lax
from jax.experimental import pallas as pl
from jax.experimental.pallas import tpu as pltpu
from jax.sharding import PartitionSpec as P

MESH = pl.DeviceIdType.MESH
NB = 32
LANES = 128
CPD = 8
NY = 8
SEQ = NB * LANES
TAPS = 2 * LANES


def leaf_angles(theta, length):
    if length == 1:
        return [theta]
    return leaf_angles(theta / 2, length // 2) + leaf_angles(theta / 2 + math.pi, length // 2)


@functools.cache
def tables():
    order = np.array([round((a * 64 / (2 * math.pi) - 0.5) / 2) % NB for a in leaf_angles(math.pi / 2, NB)])
    r = np.arange(LANES)
    angle = 2 * math.pi * (2 * order[:, None] + 0.5) * r[None, :] / (2 * SEQ)
    turn = 2 * math.pi * (r[:, None] * r[None, :] % LANES) / LANES
    c, s = np.cos(turn), np.sin(turn)
    w = np.block([[c, -s], [s, c]]).astype(np.float32)
    w_hi = w.astype(jnp.bfloat16)
    w_lo = (w - w_hi.astype(np.float32)).astype(jnp.bfloat16)
    return (
        np.cos(angle).astype(np.float32)[:, None, :],
        np.sin(angle).astype(np.float32)[:, None, :],
        w_hi,
        w_lo,
    )


def evaluate(re, im, theta):
    length = re.shape[0]
    if length == 1:
        return [(re, im)]
    half = length // 2
    c, s = math.cos(theta / 2), math.sin(theta / 2)
    if im is None:
        t_re, t_im = c * re[half:], -s * re[half:]
        low = (re[:half] + t_re, t_im)
        high = (re[:half] - t_re, -t_im)
    else:
        t_re = c * re[half:] + s * im[half:]
        t_im = c * im[half:] - s * re[half:]
        low = (re[:half] + t_re, im[:half] + t_im)
        high = (re[:half] - t_re, im[:half] - t_im)
    return evaluate(*low, theta / 2) + evaluate(*high, theta / 2 + math.pi)


def gather_back(re, im, theta, real_only):
    length = re.shape[0]
    if length == 1:
        return re, im
    half = length // 2
    a_re, a_im = gather_back(re[:half], im[:half], theta / 2, False)
    b_re, b_im = gather_back(re[half:], im[half:], theta / 2 + math.pi, False)
    c, s = math.cos(theta / 2), math.sin(theta / 2)
    d_re, d_im = a_re - b_re, a_im - b_im
    top = c * d_re - s * d_im
    if real_only:
        return jnp.concatenate([a_re + b_re, top], axis=0), None
    return jnp.concatenate([a_re + b_re, top], axis=0), jnp.concatenate([a_im + b_im, c * d_im + s * d_re], axis=0)


def lane_transform(left, right, w_hi, w_lo):
    joined = jnp.concatenate([left, right], axis=1)
    hi = joined.astype(jnp.bfloat16)
    lo = (joined - hi.astype(jnp.float32)).astype(jnp.bfloat16)
    dot = functools.partial(jnp.dot, preferred_element_type=jnp.float32)
    out = dot(hi, w_hi[...]) + (dot(lo, w_hi[...]) + dot(hi, w_lo[...]))
    return out[:, :LANES], out[:, LANES:]


def forward(x, tcos, tsin, w_hi, w_lo):
    leaves = evaluate(x, None, math.pi / 2)
    re = jnp.concatenate([leaf[0] for leaf in leaves], axis=0)
    im = jnp.concatenate([leaf[1] for leaf in leaves], axis=0)
    c, s = tcos[...], tsin[...]
    flat = (NB * CPD, LANES)
    return lane_transform((re * c + im * s).reshape(flat), (im * c - re * s).reshape(flat), w_hi, w_lo)


def inverse(re, im, tcos, tsin, w_hi, w_lo):
    b_im, b_re = lane_transform(im, re, w_hi, w_lo)
    b_im, b_re = b_im.reshape(NB, CPD, LANES), b_re.reshape(NB, CPD, LANES)
    c, s = tcos[...], tsin[...]
    return gather_back(b_re * c - b_im * s, b_im * c + b_re * s, math.pi / 2, True)[0]


def conj_mul(a, b):
    return a[0] * b[0] + a[1] * b[1], a[1] * b[0] - a[0] * b[1]


def kernel(
    values, in_gate, out_gate, target, tap_param, skip, tcos_h, tsin_h, whi_h, wlo_h,
    back, tap_parts,
    v_val, v_gate, tcos, tsin, w_hi, w_lo, tap_block,
    mix_send, mix, goal_send, goal, taps, grad, back_send, tap_send,
    load_sem, send_sem, recv_sem,
):
    me_d, me = lax.axis_index("dp"), lax.axis_index("context")
    mz, my = me_d // NY, me_d % NY
    other = (1 - mz) * NY + my
    owned = (me + NB // 2) % NB
    barrier = pltpu.get_barrier_semaphore()

    def partner(j):
        return lax.rem(me + 1 + j, NB)

    def turn(p):
        return lax.rem(p + NB // 2, NB)

    def partner_y(k):
        return lax.rem(my + 4 + k + (k > 3), NY)

    def greet(j, carry):
        pl.semaphore_signal(barrier, inc=1, device_id=(me_d, partner(j)), device_id_type=MESH)
        return carry

    def greet_y(k, carry):
        pl.semaphore_signal(barrier, inc=1, device_id=(mz * NY + partner_y(k), me), device_id_type=MESH)
        return carry

    lax.fori_loop(0, NY - 1, greet_y, 0)
    pl.semaphore_signal(barrier, inc=1, device_id=(other, owned), device_id_type=MESH)
    lax.fori_loop(0, NB - 1, greet, 0)

    loads = [
        (values, v_val),
        (in_gate, v_gate),
        (out_gate, goal_send.at[:, 0]),
        (target, goal_send.at[:, 1]),
        (tcos_h, tcos),
        (tsin_h, tsin),
        (whi_h, w_hi),
        (wlo_h, w_lo),
        (tap_param, tap_block),
    ]
    loads = [pltpu.make_async_copy(src, dst, load_sem.at[k]) for k, (src, dst) in enumerate(loads)]
    for load in loads[-1:] + loads[:-1]:
        load.start()
    pl.semaphore_wait(barrier, NB - 1 + NY - 1 + 1)

    def remote(src, dst, k, device):
        return pltpu.make_async_remote_copy(
            src_ref=src, dst_ref=dst, send_sem=send_sem.at[k], recv_sem=recv_sem.at[k], device_id=device, device_id_type=MESH
        )

    def whole(ref, k):
        return remote(ref, ref, k, (other, me))

    def spread(make, k):
        def step(j, carry):
            p = partner(j)
            src, dst = make(p)
            remote(src, dst, k, (me_d, p)).start()
            return carry

        lax.fori_loop(0, NB - 1, step, 0)

    def spread_y(make, k):
        def step(j, carry):
            y = partner_y(j)
            src, dst = make(y)
            remote(src, dst, k, (mz * NY + y, me)).start()
            return carry

        lax.fori_loop(0, NY - 1, step, 0)

    loads[8].wait()


    @pl.when(mz == 0)
    def _():
        for z in range(2):
            remote(tap_block, taps.at[0, my], 6 * z, (z * NY + my, owned)).start()

    @pl.when(mz == 1)
    def _():
        for z in range(2):
            remote(tap_block, taps.at[1, my], 6 - 6 * z, (z * NY + my, owned)).start()

    for load in loads[:2]:
        load.wait()
    mix_send[...] = v_val[...] * v_gate[...]
    for load in loads[2:4]:
        load.wait()
    spread(lambda p: (mix_send.at[turn(p)], mix.at[me]), 1)
    whole(taps.at[mz, my], 0).wait()
    spread_y(lambda y: (taps.at[mz, my], taps.at[mz, my]), 2)
    spread(lambda p: (goal_send.at[turn(p)], goal.at[me]), 7)
    whole(taps.at[1 - mz, my], 6).wait()
    spread_y(lambda y: (taps.at[1 - mz, my], taps.at[1 - mz, my]), 3)
    mix[me] = mix_send[owned]
    goal[me] = goal_send[owned]
    for load in loads[4:8]:
        load.wait()

    row = lax.broadcasted_iota(jnp.int32, (CPD, LANES), 0)
    skip_tile = jnp.zeros((CPD, LANES), jnp.float32)
    for c in range(CPD):
        skip_tile = jnp.where(row == c, skip[owned * CPD + c], skip_tile)

    lane_args = (tcos, tsin, w_hi, w_lo)
    whole(mix.at[pl.ds(0, NB - 1)], 1).wait()
    mixed = mix[...]
    mix_spec = forward(mixed, *lane_args)
    whole(taps.at[0, pl.ds(0, NY - 1)], 2).wait()
    whole(taps.at[0, pl.ds(0, NY - 1)], 3).wait()
    tap_all = taps[...].reshape(2 * NY, CPD, TAPS)
    tap_all = jnp.stack([tap_all[:, :, :LANES], tap_all[:, :, LANES:]], axis=1).reshape(NB, CPD, LANES)
    tap_spec = forward(tap_all * (SEQ**-0.5 / SEQ), *lane_args)
    product = (
        mix_spec[0] * tap_spec[0] - mix_spec[1] * tap_spec[1],
        mix_spec[0] * tap_spec[1] + mix_spec[1] * tap_spec[0],
    )
    grad[...] = inverse(*product, *lane_args) + skip_tile * mixed

    whole(goal.at[pl.ds(0, NB - 1)], 7).wait()
    gate = goal[:, 0]
    grad_out = gate * (gate * grad[...] - goal[:, 1])
    grad[...] = grad_out
    grad_spec = forward(grad_out, *lane_args)

    def spread_lags(z):
        def step(k, carry):
            y = lax.rem(my + 4 + k, NY)
            remote(tap_send.at[y, z], tap_parts.at[me_d], 4, (z * NY + y, owned)).start()
            return carry

        lax.fori_loop(0, NY, step, 0)

    tap_part = inverse(*conj_mul(grad_spec, mix_spec), *lane_args).reshape(2, NY, 2, CPD, LANES)
    for z in range(2):
        for half in range(2):
            tap_send[:, z, :, half * LANES : (half + 1) * LANES] = tap_part[z, :, half]

    back_send[...] = inverse(*conj_mul(grad_spec, tap_spec), *lane_args) + skip_tile * grad[...]

    @pl.when(mz == 1)
    def _():
        spread_lags(0)

    spread(lambda p: (back_send.at[p], back.at[owned]), 5)

    @pl.when(mz == 0)
    def _():
        spread_lags(0)

    spread_lags(1)
    keep = pltpu.make_async_copy(back_send.at[me], back.at[owned], load_sem.at[0])
    keep.start()

    whole(tap_parts, 4).wait()
    keep.wait()
    whole(back.at[pl.ds(0, NB - 1)], 5).wait()


def finish_kernel(back, in_gate, tap_parts, grad_values, tap_grad):
    grad_values[...] = in_gate[...] * back[...]
    tap_grad[...] = jnp.sum(tap_parts[...], axis=0) * ((SEQ * 2 * NY) ** -0.5 / SEQ)


def body(values, in_gate, out_gate, target, tap_param, skip):
    f32, bf16 = jnp.float32, jnp.bfloat16
    block = (NB, CPD, LANES)
    shape = values.shape
    hbm = pl.BlockSpec(memory_space=pl.ANY)
    vmem = pl.BlockSpec(memory_space=pltpu.VMEM)
    constants = [jnp.asarray(t) for t in tables()]
    values, in_gate, out_gate, target = [a.reshape(block) for a in (values, in_gate, out_gate, target)]
    tap_shape = jax.ShapeDtypeStruct(tap_param.shape, f32)
    back, tap_parts = pl.pallas_call(
        kernel,
        out_shape=(jax.ShapeDtypeStruct(block, f32), jax.ShapeDtypeStruct((2 * NY, CPD, TAPS), f32)),
        in_specs=[hbm] * 5 + [pl.BlockSpec(memory_space=pltpu.SMEM)] + [hbm] * 4,
        out_specs=(hbm, hbm),
        scratch_shapes=[
            pltpu.VMEM(block, f32),
            pltpu.VMEM(block, f32),
            pltpu.VMEM((NB, 1, LANES), f32),
            pltpu.VMEM((NB, 1, LANES), f32),
            pltpu.VMEM((2 * LANES, 2 * LANES), bf16),
            pltpu.VMEM((2 * LANES, 2 * LANES), bf16),
            pltpu.VMEM((CPD, TAPS), f32),
            pltpu.VMEM(block, f32),
            pltpu.VMEM(block, f32),
            pltpu.VMEM((NB, 2, CPD, LANES), f32),
            pltpu.VMEM((NB, 2, CPD, LANES), f32),
            pltpu.VMEM((2, NY, CPD, TAPS), f32),
            pltpu.VMEM(block, f32),
            pltpu.VMEM(block, f32),
            pltpu.VMEM((NY, 2, CPD, TAPS), f32),
            pltpu.SemaphoreType.DMA((9,)),
            pltpu.SemaphoreType.DMA((8,)),
            pltpu.SemaphoreType.DMA((8,)),
        ],
        compiler_params=pltpu.CompilerParams(collective_id=0, has_side_effects=True, vmem_limit_bytes=56 * 1024 * 1024),
        cost_estimate=pl.CostEstimate(flops=2**30, bytes_accessed=2**20, transcendentals=0),
        name="gated_conv",
    )(values, in_gate, out_gate, target, tap_param, skip, *constants)
    grad_values, tap_grad = pl.pallas_call(
        finish_kernel,
        out_shape=(jax.ShapeDtypeStruct(block, f32), tap_shape),
        in_specs=[vmem] * 3,
        out_specs=(vmem, vmem),
        name="finish",
    )(back, in_gate, tap_parts)
    return grad_values.reshape(shape), tap_grad


def solution(mesh):
    stream = P("dp", None, "context")
    return jax.shard_map(
        body,
        mesh=mesh,
        in_specs=(stream, stream, stream, stream, P("context", "dp"), P()),
        out_specs=(stream, P("context", "dp")),
        check_vma=False,
    )
```

```python
import functools
import math

import jax
import jax.numpy as jnp
import numpy as np
from jax import lax
from jax.experimental import pallas as pl
from jax.experimental.pallas import tpu as pltpu
from jax.sharding import PartitionSpec as P

MESH = pl.DeviceIdType.MESH
NB = 32
LANES = 128
CPD = 8
NY = 8
SEQ = NB * LANES
TAPS = 2 * LANES


def leaf_angles(theta, length):
    if length == 1:
        return [theta]
    return leaf_angles(theta / 2, length // 2) + leaf_angles(theta / 2 + math.pi, length // 2)


@functools.cache
def tables():
    order = np.array([round((a * 64 / (2 * math.pi) - 0.5) / 2) % NB for a in leaf_angles(math.pi / 2, NB)])
    r = np.arange(LANES)
    angle = 2 * math.pi * (2 * order[:, None] + 0.5) * r[None, :] / (2 * SEQ)
    turn = 2 * math.pi * (r[:, None] * r[None, :] % LANES) / LANES
    c, s = np.cos(turn), np.sin(turn)
    w = np.block([[c, -s], [s, c]]).astype(np.float32)
    w_hi = w.astype(jnp.bfloat16)
    w_lo = (w - w_hi.astype(np.float32)).astype(jnp.bfloat16)
    return (
        np.cos(angle).astype(np.float32)[:, None, :],
        np.sin(angle).astype(np.float32)[:, None, :],
        w_hi,
        w_lo,
    )


def evaluate(re, im, theta):
    length = re.shape[0]
    if length == 1:
        return [(re, im)]
    half = length // 2
    c, s = math.cos(theta / 2), math.sin(theta / 2)
    if im is None:
        t_re, t_im = c * re[half:], -s * re[half:]
        low = (re[:half] + t_re, t_im)
        high = (re[:half] - t_re, -t_im)
    else:
        t_re = c * re[half:] + s * im[half:]
        t_im = c * im[half:] - s * re[half:]
        low = (re[:half] + t_re, im[:half] + t_im)
        high = (re[:half] - t_re, im[:half] - t_im)
    return evaluate(*low, theta / 2) + evaluate(*high, theta / 2 + math.pi)


def gather_back(re, im, theta, real_only):
    length = re.shape[0]
    if length == 1:
        return re, im
    half = length // 2
    a_re, a_im = gather_back(re[:half], im[:half], theta / 2, False)
    b_re, b_im = gather_back(re[half:], im[half:], theta / 2 + math.pi, False)
    c, s = math.cos(theta / 2), math.sin(theta / 2)
    d_re, d_im = a_re - b_re, a_im - b_im
    top = c * d_re - s * d_im
    if real_only:
        return jnp.concatenate([a_re + b_re, top], axis=0), None
    return jnp.concatenate([a_re + b_re, top], axis=0), jnp.concatenate([a_im + b_im, c * d_im + s * d_re], axis=0)


def lane_transform(left, right, w_hi, w_lo):
    joined = jnp.concatenate([left, right], axis=1)
    hi = joined.astype(jnp.bfloat16)
    lo = (joined - hi.astype(jnp.float32)).astype(jnp.bfloat16)
    dot = functools.partial(jnp.dot, preferred_element_type=jnp.float32)
    out = dot(hi, w_hi[...]) + (dot(lo, w_hi[...]) + dot(hi, w_lo[...]))
    return out[:, :LANES], out[:, LANES:]


def forward(x, tcos, tsin, w_hi, w_lo):
    leaves = evaluate(x, None, math.pi / 2)
    re = jnp.concatenate([leaf[0] for leaf in leaves], axis=0)
    im = jnp.concatenate([leaf[1] for leaf in leaves], axis=0)
    c, s = tcos[...], tsin[...]
    flat = (NB * CPD, LANES)
    return lane_transform((re * c + im * s).reshape(flat), (im * c - re * s).reshape(flat), w_hi, w_lo)


def inverse(re, im, tcos, tsin, w_hi, w_lo):
    b_im, b_re = lane_transform(im, re, w_hi, w_lo)
    b_im, b_re = b_im.reshape(NB, CPD, LANES), b_re.reshape(NB, CPD, LANES)
    c, s = tcos[...], tsin[...]
    return gather_back(b_re * c - b_im * s, b_im * c + b_re * s, math.pi / 2, True)[0]


def conj_mul(a, b):
    return a[0] * b[0] + a[1] * b[1], a[1] * b[0] - a[0] * b[1]


def kernel(
    values, in_gate, out_gate, target, tap_param, skip, tcos_h, tsin_h, whi_h, wlo_h,
    back, tap_parts,
    v_val, v_gate, tcos, tsin, w_hi, w_lo, tap_block,
    mix_send, mix, goal_send, goal, taps, grad, back_send, tap_send,
    load_sem, send_sem, recv_sem,
):
    me_d, me = lax.axis_index("dp"), lax.axis_index("context")
    mz, my = me_d // NY, me_d % NY
    other = (1 - mz) * NY + my
    owned = (me + NB // 2) % NB
    barrier = pltpu.get_barrier_semaphore()

    def partner(j):
        return lax.rem(me + 1 + j, NB)

    def turn(p):
        return lax.rem(p + NB // 2, NB)

    def partner_y(k):
        return lax.rem(my + 4 + k + (k > 3), NY)

    def greet(j, carry):
        pl.semaphore_signal(barrier, inc=1, device_id=(me_d, partner(j)), device_id_type=MESH)
        return carry

    def greet_y(k, carry):
        pl.semaphore_signal(barrier, inc=1, device_id=(mz * NY + partner_y(k), me), device_id_type=MESH)
        return carry

    lax.fori_loop(0, NY - 1, greet_y, 0)
    pl.semaphore_signal(barrier, inc=1, device_id=(other, owned), device_id_type=MESH)
    lax.fori_loop(0, NB - 1, greet, 0)

    loads = [
        (values, v_val),
        (in_gate, v_gate),
        (out_gate, goal_send.at[:, 0]),
        (target, goal_send.at[:, 1]),
        (tcos_h, tcos),
        (tsin_h, tsin),
        (whi_h, w_hi),
        (wlo_h, w_lo),
        (tap_param, tap_block),
    ]
    loads = [pltpu.make_async_copy(src, dst, load_sem.at[k]) for k, (src, dst) in enumerate(loads)]
    for load in loads[-1:] + loads[:-1]:
        load.start()
    pl.semaphore_wait(barrier, NB - 1 + NY - 1 + 1)

    def remote(src, dst, k, device):
        return pltpu.make_async_remote_copy(
            src_ref=src, dst_ref=dst, send_sem=send_sem.at[k], recv_sem=recv_sem.at[k], device_id=device, device_id_type=MESH
        )

    def whole(ref, k):
        return remote(ref, ref, k, (other, me))

    def spread(make, k):
        def step(j, carry):
            p = partner(j)
            src, dst = make(p)
            remote(src, dst, k, (me_d, p)).start()
            return carry

        lax.fori_loop(0, NB - 1, step, 0)

    def spread_y(make, k):
        def step(j, carry):
            y = partner_y(j)
            src, dst = make(y)
            remote(src, dst, k, (mz * NY + y, me)).start()
            return carry

        lax.fori_loop(0, NY - 1, step, 0)

    loads[8].wait()


    @pl.when(mz == 0)
    def _():
        for z in range(2):
            remote(tap_block, taps.at[0, my], 6 * z, (z * NY + my, owned)).start()

    @pl.when(mz == 1)
    def _():
        for z in range(2):
            remote(tap_block, taps.at[1, my], 6 - 6 * z, (z * NY + my, owned)).start()

    for load in loads[:2]:
        load.wait()
    mix_send[...] = v_val[...] * v_gate[...]
    for load in loads[2:4]:
        load.wait()
    spread(lambda p: (mix_send.at[turn(p)], mix.at[me]), 1)
    whole(taps.at[mz, my], 0).wait()
    spread_y(lambda y: (taps.at[mz, my], taps.at[mz, my]), 2)
    spread(lambda p: (goal_send.at[turn(p)], goal.at[me]), 7)
    whole(taps.at[1 - mz, my], 6).wait()
    spread_y(lambda y: (taps.at[1 - mz, my], taps.at[1 - mz, my]), 3)
    mix[me] = mix_send[owned]
    goal[me] = goal_send[owned]
    for load in loads[4:8]:
        load.wait()

    row = lax.broadcasted_iota(jnp.int32, (CPD, LANES), 0)
    skip_tile = jnp.zeros((CPD, LANES), jnp.float32)
    for c in range(CPD):
        skip_tile = jnp.where(row == c, skip[owned * CPD + c], skip_tile)

    lane_args = (tcos, tsin, w_hi, w_lo)
    whole(mix.at[pl.ds(0, NB - 1)], 1).wait()
    mixed = mix[...]
    mix_spec = forward(mixed, *lane_args)
    whole(taps.at[0, pl.ds(0, NY - 1)], 2).wait()
    whole(taps.at[0, pl.ds(0, NY - 1)], 3).wait()
    tap_all = taps[...].reshape(2 * NY, CPD, TAPS)
    tap_all = jnp.stack([tap_all[:, :, :LANES], tap_all[:, :, LANES:]], axis=1).reshape(NB, CPD, LANES)
    tap_spec = forward(tap_all * (SEQ**-0.5 / SEQ), *lane_args)
    product = (
        mix_spec[0] * tap_spec[0] - mix_spec[1] * tap_spec[1],
        mix_spec[0] * tap_spec[1] + mix_spec[1] * tap_spec[0],
    )
    grad[...] = inverse(*product, *lane_args) + skip_tile * mixed

    whole(goal.at[pl.ds(0, NB - 1)], 7).wait()
    gate = goal[:, 0]
    grad_out = gate * (gate * grad[...] - goal[:, 1])
    grad[...] = grad_out
    grad_spec = forward(grad_out, *lane_args)

    def spread_lags(z):
        def step(k, carry):
            y = k
            remote(tap_send.at[y, z], tap_parts.at[me_d], 4, (z * NY + y, owned)).start()
            return carry

        lax.fori_loop(0, NY, step, 0)

    tap_part = inverse(*conj_mul(grad_spec, mix_spec), *lane_args).reshape(2, NY, 2, CPD, LANES)
    for z in range(2):
        for half in range(2):
            tap_send[:, z, :, half * LANES : (half + 1) * LANES] = tap_part[z, :, half]

    back_send[...] = inverse(*conj_mul(grad_spec, tap_spec), *lane_args) + skip_tile * grad[...]

    @pl.when(mz == 1)
    def _():
        spread_lags(0)


    def spread_back(j, carry):
        p = lax.div(j, 8) * 8 + lax.rem(me + 1 + j, 8)

        @pl.when(p != me)
        def _():
            remote(back_send.at[p], back.at[owned], 5, (me_d, p)).start()

        return carry

    lax.fori_loop(0, NB, spread_back, 0)

    @pl.when(mz == 0)
    def _():
        spread_lags(0)

    spread_lags(1)
    keep = pltpu.make_async_copy(back_send.at[me], back.at[owned], load_sem.at[0])
    keep.start()

    whole(tap_parts, 4).wait()
    keep.wait()
    whole(back.at[pl.ds(0, NB - 1)], 5).wait()


def finish_kernel(back, in_gate, tap_parts, grad_values, tap_grad):
    grad_values[...] = in_gate[...] * back[...]
    tap_grad[...] = jnp.sum(tap_parts[...], axis=0) * ((SEQ * 2 * NY) ** -0.5 / SEQ)


def body(values, in_gate, out_gate, target, tap_param, skip):
    f32, bf16 = jnp.float32, jnp.bfloat16
    block = (NB, CPD, LANES)
    shape = values.shape
    hbm = pl.BlockSpec(memory_space=pl.ANY)
    vmem = pl.BlockSpec(memory_space=pltpu.VMEM)
    constants = [jnp.asarray(t) for t in tables()]
    values, in_gate, out_gate, target = [a.reshape(block) for a in (values, in_gate, out_gate, target)]
    tap_shape = jax.ShapeDtypeStruct(tap_param.shape, f32)
    back, tap_parts = pl.pallas_call(
        kernel,
        out_shape=(jax.ShapeDtypeStruct(block, f32), jax.ShapeDtypeStruct((2 * NY, CPD, TAPS), f32)),
        in_specs=[hbm] * 5 + [pl.BlockSpec(memory_space=pltpu.SMEM)] + [hbm] * 4,
        out_specs=(hbm, hbm),
        scratch_shapes=[
            pltpu.VMEM(block, f32),
            pltpu.VMEM(block, f32),
            pltpu.VMEM((NB, 1, LANES), f32),
            pltpu.VMEM((NB, 1, LANES), f32),
            pltpu.VMEM((2 * LANES, 2 * LANES), bf16),
            pltpu.VMEM((2 * LANES, 2 * LANES), bf16),
            pltpu.VMEM((CPD, TAPS), f32),
            pltpu.VMEM(block, f32),
            pltpu.VMEM(block, f32),
            pltpu.VMEM((NB, 2, CPD, LANES), f32),
            pltpu.VMEM((NB, 2, CPD, LANES), f32),
            pltpu.VMEM((2, NY, CPD, TAPS), f32),
            pltpu.VMEM(block, f32),
            pltpu.VMEM(block, f32),
            pltpu.VMEM((NY, 2, CPD, TAPS), f32),
            pltpu.SemaphoreType.DMA((9,)),
            pltpu.SemaphoreType.DMA((8,)),
            pltpu.SemaphoreType.DMA((8,)),
        ],
        compiler_params=pltpu.CompilerParams(collective_id=0, has_side_effects=True, vmem_limit_bytes=56 * 1024 * 1024),
        cost_estimate=pl.CostEstimate(flops=2**30, bytes_accessed=2**20, transcendentals=0),
        name="gated_conv",
    )(values, in_gate, out_gate, target, tap_param, skip, *constants)
    grad_values, tap_grad = pl.pallas_call(
        finish_kernel,
        out_shape=(jax.ShapeDtypeStruct(block, f32), tap_shape),
        in_specs=[vmem] * 3,
        out_specs=(vmem, vmem),
        name="finish",
    )(back, in_gate, tap_parts)
    return grad_values.reshape(shape), tap_grad


def solution(mesh):
    stream = P("dp", None, "context")
    return jax.shard_map(
        body,
        mesh=mesh,
        in_specs=(stream, stream, stream, stream, P("context", "dp"), P()),
        out_specs=(stream, P("context", "dp")),
        check_vma=False,
    )
```

```python
import functools
import math

import jax
import jax.numpy as jnp
import numpy as np
from jax import lax
from jax.experimental import pallas as pl
from jax.experimental.pallas import tpu as pltpu
from jax.sharding import PartitionSpec as P

MESH = pl.DeviceIdType.MESH
NB = 32
LANES = 128
CPD = 8
NY = 8
SEQ = NB * LANES
TAPS = 2 * LANES


def leaf_angles(theta, length):
    if length == 1:
        return [theta]
    return leaf_angles(theta / 2, length // 2) + leaf_angles(theta / 2 + math.pi, length // 2)


@functools.cache
def tables():
    order = np.array([round((a * 64 / (2 * math.pi) - 0.5) / 2) % NB for a in leaf_angles(math.pi / 2, NB)])
    r = np.arange(LANES)
    angle = 2 * math.pi * (2 * order[:, None] + 0.5) * r[None, :] / (2 * SEQ)
    turn = 2 * math.pi * (r[:, None] * r[None, :] % LANES) / LANES
    c, s = np.cos(turn), np.sin(turn)
    w = np.block([[c, -s], [s, c]]).astype(np.float32)
    w_hi = w.astype(jnp.bfloat16)
    w_lo = (w - w_hi.astype(np.float32)).astype(jnp.bfloat16)
    return (
        np.cos(angle).astype(np.float32)[:, None, :],
        np.sin(angle).astype(np.float32)[:, None, :],
        w_hi,
        w_lo,
    )


def evaluate(re, im, theta):
    length = re.shape[0]
    if length == 1:
        return [(re, im)]
    half = length // 2
    c, s = math.cos(theta / 2), math.sin(theta / 2)
    if im is None:
        t_re, t_im = c * re[half:], -s * re[half:]
        low = (re[:half] + t_re, t_im)
        high = (re[:half] - t_re, -t_im)
    else:
        t_re = c * re[half:] + s * im[half:]
        t_im = c * im[half:] - s * re[half:]
        low = (re[:half] + t_re, im[:half] + t_im)
        high = (re[:half] - t_re, im[:half] - t_im)
    return evaluate(*low, theta / 2) + evaluate(*high, theta / 2 + math.pi)


def gather_back(re, im, theta, real_only):
    length = re.shape[0]
    if length == 1:
        return re, im
    half = length // 2
    a_re, a_im = gather_back(re[:half], im[:half], theta / 2, False)
    b_re, b_im = gather_back(re[half:], im[half:], theta / 2 + math.pi, False)
    c, s = math.cos(theta / 2), math.sin(theta / 2)
    d_re, d_im = a_re - b_re, a_im - b_im
    top = c * d_re - s * d_im
    if real_only:
        return jnp.concatenate([a_re + b_re, top], axis=0), None
    return jnp.concatenate([a_re + b_re, top], axis=0), jnp.concatenate([a_im + b_im, c * d_im + s * d_re], axis=0)


def lane_transform(left, right, w_hi, w_lo):
    joined = jnp.concatenate([left, right], axis=1)
    hi = joined.astype(jnp.bfloat16)
    lo = (joined - hi.astype(jnp.float32)).astype(jnp.bfloat16)
    dot = functools.partial(jnp.dot, preferred_element_type=jnp.float32)
    out = dot(hi, w_hi[...]) + (dot(lo, w_hi[...]) + dot(hi, w_lo[...]))
    return out[:, :LANES], out[:, LANES:]


def forward(x, tcos, tsin, w_hi, w_lo):
    leaves = evaluate(x, None, math.pi / 2)
    re = jnp.concatenate([leaf[0] for leaf in leaves], axis=0)
    im = jnp.concatenate([leaf[1] for leaf in leaves], axis=0)
    c, s = tcos[...], tsin[...]
    flat = (NB * CPD, LANES)
    return lane_transform((re * c + im * s).reshape(flat), (im * c - re * s).reshape(flat), w_hi, w_lo)


def inverse(re, im, tcos, tsin, w_hi, w_lo):
    b_im, b_re = lane_transform(im, re, w_hi, w_lo)
    b_im, b_re = b_im.reshape(NB, CPD, LANES), b_re.reshape(NB, CPD, LANES)
    c, s = tcos[...], tsin[...]
    return gather_back(b_re * c - b_im * s, b_im * c + b_re * s, math.pi / 2, True)[0]


def conj_mul(a, b):
    return a[0] * b[0] + a[1] * b[1], a[1] * b[0] - a[0] * b[1]


def kernel(
    values, in_gate, out_gate, target, tap_param, skip, tcos_h, tsin_h, whi_h, wlo_h,
    back, tap_parts,
    v_val, v_gate, tcos, tsin, w_hi, w_lo, tap_block,
    mix_send, mix, goal_send, goal, taps, grad, back_send, tap_send,
    load_sem, send_sem, recv_sem,
):
    me_d, me = lax.axis_index("dp"), lax.axis_index("context")
    mz, my = me_d // NY, me_d % NY
    other = (1 - mz) * NY + my
    owned = (me + NB // 2) % NB
    barrier = pltpu.get_barrier_semaphore()

    def partner(j):
        return lax.rem(me + 1 + j, NB)

    def turn(p):
        return lax.rem(p + NB // 2, NB)

    def partner_y(k):
        return lax.rem(my + 4 + k + (k > 3), NY)

    def greet(j, carry):
        pl.semaphore_signal(barrier, inc=1, device_id=(me_d, partner(j)), device_id_type=MESH)
        return carry

    def greet_y(k, carry):
        pl.semaphore_signal(barrier, inc=1, device_id=(mz * NY + partner_y(k), me), device_id_type=MESH)
        return carry

    lax.fori_loop(0, NY - 1, greet_y, 0)
    pl.semaphore_signal(barrier, inc=1, device_id=(other, owned), device_id_type=MESH)
    lax.fori_loop(0, NB - 1, greet, 0)

    loads = [
        (values, v_val),
        (in_gate, v_gate),
        (out_gate, goal_send.at[:, 0]),
        (target, goal_send.at[:, 1]),
        (tcos_h, tcos),
        (tsin_h, tsin),
        (whi_h, w_hi),
        (wlo_h, w_lo),
        (tap_param, tap_block),
    ]
    loads = [pltpu.make_async_copy(src, dst, load_sem.at[k]) for k, (src, dst) in enumerate(loads)]
    for load in loads[-1:] + loads[:-1]:
        load.start()
    pl.semaphore_wait(barrier, NB - 1 + NY - 1 + 1)

    def remote(src, dst, k, device):
        return pltpu.make_async_remote_copy(
            src_ref=src, dst_ref=dst, send_sem=send_sem.at[k], recv_sem=recv_sem.at[k], device_id=device, device_id_type=MESH
        )

    def whole(ref, k):
        return remote(ref, ref, k, (other, me))

    def spread(make, k):
        def step(j, carry):
            p = partner(j)
            src, dst = make(p)
            remote(src, dst, k, (me_d, p)).start()
            return carry

        lax.fori_loop(0, NB - 1, step, 0)

    def spread_y(make, k):
        def step(j, carry):
            y = partner_y(j)
            src, dst = make(y)
            remote(src, dst, k, (mz * NY + y, me)).start()
            return carry

        lax.fori_loop(0, NY - 1, step, 0)

    loads[8].wait()


    @pl.when(mz == 0)
    def _():
        for z in range(2):
            remote(tap_block, taps.at[0, my], 6 * z, (z * NY + my, owned)).start()

    @pl.when(mz == 1)
    def _():
        for z in range(2):
            remote(tap_block, taps.at[1, my], 6 - 6 * z, (z * NY + my, owned)).start()

    for load in loads[:2]:
        load.wait()
    mix_send[...] = v_val[...] * v_gate[...]
    spread(lambda p: (mix_send.at[turn(p)], mix.at[me]), 1)
    whole(taps.at[mz, my], 0).wait()
    spread_y(lambda y: (taps.at[mz, my], taps.at[mz, my]), 2)
    for load in loads[2:4]:
        load.wait()
    spread(lambda p: (goal_send.at[turn(p)], goal.at[me]), 7)
    whole(taps.at[1 - mz, my], 6).wait()
    spread_y(lambda y: (taps.at[1 - mz, my], taps.at[1 - mz, my]), 3)
    mix[me] = mix_send[owned]
    goal[me] = goal_send[owned]
    for load in loads[4:8]:
        load.wait()

    row = lax.broadcasted_iota(jnp.int32, (CPD, LANES), 0)
    skip_tile = jnp.zeros((CPD, LANES), jnp.float32)
    for c in range(CPD):
        skip_tile = jnp.where(row == c, skip[owned * CPD + c], skip_tile)

    lane_args = (tcos, tsin, w_hi, w_lo)
    whole(mix.at[pl.ds(0, NB - 1)], 1).wait()
    mixed = mix[...]
    mix_spec = forward(mixed, *lane_args)
    whole(taps.at[0, pl.ds(0, NY - 1)], 2).wait()
    whole(taps.at[0, pl.ds(0, NY - 1)], 3).wait()
    tap_all = taps[...].reshape(2 * NY, CPD, TAPS)
    tap_all = jnp.stack([tap_all[:, :, :LANES], tap_all[:, :, LANES:]], axis=1).reshape(NB, CPD, LANES)
    tap_spec = forward(tap_all * (SEQ**-0.5 / SEQ), *lane_args)
    product = (
        mix_spec[0] * tap_spec[0] - mix_spec[1] * tap_spec[1],
        mix_spec[0] * tap_spec[1] + mix_spec[1] * tap_spec[0],
    )
    grad[...] = inverse(*product, *lane_args) + skip_tile * mixed

    whole(goal.at[pl.ds(0, NB - 1)], 7).wait()
    gate = goal[:, 0]
    grad_out = gate * (gate * grad[...] - goal[:, 1])
    grad[...] = grad_out
    grad_spec = forward(grad_out, *lane_args)

    def spread_lags(z):
        def step(k, carry):
            y = k
            remote(tap_send.at[y, z], tap_parts.at[me_d], 4, (z * NY + y, owned)).start()
            return carry

        lax.fori_loop(0, NY, step, 0)

    tap_part = inverse(*conj_mul(grad_spec, mix_spec), *lane_args).reshape(2, NY, 2, CPD, LANES)
    for z in range(2):
        for half in range(2):
            tap_send[:, z, :, half * LANES : (half + 1) * LANES] = tap_part[z, :, half]

    back_send[...] = inverse(*conj_mul(grad_spec, tap_spec), *lane_args) + skip_tile * grad[...]

    @pl.when(mz == 1)
    def _():
        spread_lags(0)


    def spread_back(j, carry):
        p = lax.div(j, 8) * 8 + lax.rem(me + 1 + j, 8)

        @pl.when(p != me)
        def _():
            remote(back_send.at[p], back.at[owned], 5, (me_d, p)).start()

        return carry

    lax.fori_loop(0, NB, spread_back, 0)

    @pl.when(mz == 0)
    def _():
        spread_lags(0)

    spread_lags(1)
    keep = pltpu.make_async_copy(back_send.at[me], back.at[owned], load_sem.at[0])
    keep.start()

    whole(tap_parts, 4).wait()
    keep.wait()
    whole(back.at[pl.ds(0, NB - 1)], 5).wait()


def finish_kernel(back, in_gate, tap_parts, grad_values, tap_grad):
    grad_values[...] = in_gate[...] * back[...]
    tap_grad[...] = jnp.sum(tap_parts[...], axis=0) * ((SEQ * 2 * NY) ** -0.5 / SEQ)


def body(values, in_gate, out_gate, target, tap_param, skip):
    f32, bf16 = jnp.float32, jnp.bfloat16
    block = (NB, CPD, LANES)
    shape = values.shape
    hbm = pl.BlockSpec(memory_space=pl.ANY)
    vmem = pl.BlockSpec(memory_space=pltpu.VMEM)
    constants = [jnp.asarray(t) for t in tables()]
    values, in_gate, out_gate, target = [a.reshape(block) for a in (values, in_gate, out_gate, target)]
    tap_shape = jax.ShapeDtypeStruct(tap_param.shape, f32)
    back, tap_parts = pl.pallas_call(
        kernel,
        out_shape=(jax.ShapeDtypeStruct(block, f32), jax.ShapeDtypeStruct((2 * NY, CPD, TAPS), f32)),
        in_specs=[hbm] * 5 + [pl.BlockSpec(memory_space=pltpu.SMEM)] + [hbm] * 4,
        out_specs=(hbm, hbm),
        scratch_shapes=[
            pltpu.VMEM(block, f32),
            pltpu.VMEM(block, f32),
            pltpu.VMEM((NB, 1, LANES), f32),
            pltpu.VMEM((NB, 1, LANES), f32),
            pltpu.VMEM((2 * LANES, 2 * LANES), bf16),
            pltpu.VMEM((2 * LANES, 2 * LANES), bf16),
            pltpu.VMEM((CPD, TAPS), f32),
            pltpu.VMEM(block, f32),
            pltpu.VMEM(block, f32),
            pltpu.VMEM((NB, 2, CPD, LANES), f32),
            pltpu.VMEM((NB, 2, CPD, LANES), f32),
            pltpu.VMEM((2, NY, CPD, TAPS), f32),
            pltpu.VMEM(block, f32),
            pltpu.VMEM(block, f32),
            pltpu.VMEM((NY, 2, CPD, TAPS), f32),
            pltpu.SemaphoreType.DMA((9,)),
            pltpu.SemaphoreType.DMA((8,)),
            pltpu.SemaphoreType.DMA((8,)),
        ],
        compiler_params=pltpu.CompilerParams(collective_id=0, has_side_effects=True, vmem_limit_bytes=56 * 1024 * 1024),
        cost_estimate=pl.CostEstimate(flops=2**30, bytes_accessed=2**20, transcendentals=0),
        name="gated_conv",
    )(values, in_gate, out_gate, target, tap_param, skip, *constants)
    grad_values, tap_grad = pl.pallas_call(
        finish_kernel,
        out_shape=(jax.ShapeDtypeStruct(block, f32), tap_shape),
        in_specs=[vmem] * 3,
        out_specs=(vmem, vmem),
        name="finish",
    )(back, in_gate, tap_parts)
    return grad_values.reshape(shape), tap_grad


def solution(mesh):
    stream = P("dp", None, "context")
    return jax.shard_map(
        body,
        mesh=mesh,
        in_specs=(stream, stream, stream, stream, P("context", "dp"), P()),
        out_specs=(stream, P("context", "dp")),
        check_vma=False,
    )
```
